256 devices in a mesh: ctx: 32 (over z_hi, x, core), head: 8 (over z_lo, y).
Axes of the slice: x: 4, y: 4, z: 8 (z_hi: 4, z_lo: 2; z = z_hi * 2 + z_lo), core: 2. Of those that a mesh axis runs over, the one named last changes fastest.
Arguments:
- queries: bfloat16 [512, 24576], P('ctx', 'head'), may hold values from -70 to 70, as said below
- cache: bfloat16 [24576, 576], P(('ctx', 'head')), may hold values from -6 to 6, as said below
- cache_len: int32 [32], P('ctx'), may hold values from 192 to 768, as said below
- new_latents: bfloat16 [512, 576], P('ctx'), may hold values from -6 to 6
- prefix_len: int32 [1], replicated, may hold values from 1 to 511
- latent_up: bfloat16 [512, 32768], P(None, 'head'), may hold values from -0.25 to 0.25
Outputs:
- attended: bfloat16 [512, 16384], P('ctx', 'head')
The draws below stay inside these ranges and needn't reach their ends.
Inputs may be any that keep to these rules, and one draw needn't show every extreme that they name: `queries`: query entries lie in this range. `cache`: latent entries lie in this range. `cache_len`: at least 192 live positions a block; some block is full.
All inputs are finite; a program needn't handle non-finite values.
Results may differ from the reference program's by a relative error of at most 0.0071.
Values may be sent and summed in bfloat16 or wider, within the bound.
No kernel may reach another device: no remote copies, remote signals or barrier semaphores. Data moves between devices by JAX's collectives and lax.ppermute only.
A program may use at most 128 MiB of HBM per device.

```python
import jax
import jax.numpy as jnp
from jax import lax

H = 128
LATENT = 512
ROPE = 64
NOPE = 128
VDIM = 128
CTX_DEV = 768
SHARDS = 32
Q = 512
CACHE = 24576


def draw_queries(key, part):
    key = jax.random.fold_in(key, 1)
    normal_part = jnp.clip(jax.random.normal(key, (Q, H * (NOPE + ROPE)), jnp.float32) * 2.5, -15.0, 15.0)
    return normal_part.astype(jnp.bfloat16)


def draw_cache(key, part):
    key = jax.random.fold_in(key, 2)
    normal_part = jnp.clip(jax.random.normal(key, (CACHE, LATENT + ROPE), jnp.float32), -6.0, 6.0)
    return normal_part.astype(jnp.bfloat16)


def draw_cache_len(key, part):
    key = jax.random.fold_in(key, 3)
    key_len, key_full = jax.random.split(key)
    lengths = jax.random.randint(key_len, (SHARDS,), CTX_DEV // 4, CTX_DEV + 1)
    full_block = jax.random.randint(key_full, (), 0, SHARDS)
    return jnp.where(jnp.arange(SHARDS) == full_block, CTX_DEV, lengths).astype(jnp.int32)


def block_levels(rng, extent, shards, low, largest):
    gain = 1.0
    for dim, shards_of in shards:
        draws = jax.random.uniform(jax.random.fold_in(jax.random.fold_in(rng, 6), dim), (shards_of,), jnp.float32, low / len(shards), largest / len(shards))
        gain = gain * jnp.repeat(jnp.exp(draws), extent[dim] // shards_of).reshape((-1,) + (1,) * (len(extent) - 1 - dim))
    return gain


def normal_values(stream_key, extent, deviation, bound, shards=(), kind=jnp.bfloat16):
    factor_of = block_levels(stream_key, extent, shards, -0.22, 0.18) if shards else 1.0
    values = jax.random.normal(stream_key, extent, jnp.float32) * deviation * factor_of
    return jnp.minimum(jnp.maximum(values, -bound), bound).astype(kind)


def setup_inputs(seed: int = 0) -> dict:
    streams_of = jax.random.split(jax.random.key(seed), 7)
    return {
        "queries": draw_queries(jax.random.fold_in(streams_of[6], 71), 0),
        "cache": draw_cache(jax.random.fold_in(streams_of[6], 71), 0),
        "cache_len": draw_cache_len(jax.random.fold_in(streams_of[6], 71), 0),
        "new_latents": normal_values(streams_of[3], (Q, LATENT + ROPE), 1.0, 6.0, ((0, 32),)),
        "prefix_len": jax.random.randint(streams_of[4], (1,), 1, Q).astype(jnp.int32),
        "latent_up": normal_values(streams_of[5], (LATENT, H * (NOPE + VDIM)), LATENT ** -0.5, 0.25, ((1, 8),)),
    }


def to_bf16_kept(array):
    rounded = lax.optimization_barrier(array.astype(jnp.bfloat16))
    return rounded.astype(jnp.float32)


def reference(queries, cache, cache_len, new_latents, prefix_len, latent_up):
    total_rows = queries.shape[0]
    shard_count = cache_len.shape[0]
    block_span = cache.shape[0] // shard_count
    own_rows = total_rows // shard_count
    group_size = 8
    score_scale = (NOPE + ROPE) ** -0.5
    query_view = queries.reshape(total_rows, H, NOPE + ROPE)
    weight_view = latent_up.reshape(LATENT, H, NOPE + VDIM)
    cached_valid = jnp.arange(block_span, dtype=jnp.int32)[None, :] < cache_len[:, None]
    new_index = jnp.arange(total_rows, dtype=jnp.int32).reshape(shard_count, own_rows)
    query_index = jnp.arange(total_rows, dtype=jnp.int32)
    new_valid = (new_index[None] <= query_index[:, None, None]) | (new_index[None] < prefix_len[0])
    cache_content = cache[:, :LATENT].astype(jnp.float32)
    cache_rotary = cache[:, LATENT:].astype(jnp.float32)
    new_content = new_latents[:, :LATENT].astype(jnp.float32)
    new_rotary = new_latents[:, LATENT:].astype(jnp.float32)

    def one_group(group_index):
        start = (group_index * group_size).astype(jnp.int32)
        query_part = lax.dynamic_slice_in_dim(query_view, start, group_size, 1).astype(jnp.float32)
        weight_part = lax.dynamic_slice_in_dim(weight_view, start, group_size, 1).astype(jnp.float32)
        lifted_cache = to_bf16_kept(jnp.einsum("tc,chd->htd", cache_content, weight_part))
        lifted_new = to_bf16_kept(jnp.einsum("tc,chd->htd", new_content, weight_part))

        def scores_for(lifted, rotary):
            content_part = jnp.einsum("qhd,htd->hqt", query_part[:, :, :NOPE], lifted[:, :, :NOPE])
            rotary_part = jnp.einsum("qhr,tr->hqt", query_part[:, :, NOPE:], rotary)
            return (content_part + rotary_part) * score_scale

        cached_scores = scores_for(lifted_cache, cache_rotary).reshape(group_size, total_rows, shard_count, block_span)
        cached_scores = jnp.where(cached_valid[None, None], cached_scores, -jnp.inf)
        new_scores = scores_for(lifted_new, new_rotary).reshape(group_size, total_rows, shard_count, own_rows)
        new_scores = jnp.where(new_valid[None], new_scores, -jnp.inf)
        block_max = jnp.maximum(jnp.max(cached_scores, axis=-1), jnp.max(new_scores, axis=-1))
        cached_exp = jnp.exp(cached_scores - block_max[..., None])
        new_exp = jnp.exp(new_scores - block_max[..., None])
        block_total = jnp.sum(cached_exp, axis=-1) + jnp.sum(new_exp, axis=-1)
        cached_values = lifted_cache[:, :, NOPE:].reshape(group_size, shard_count, block_span, VDIM)
        new_values = lifted_new[:, :, NOPE:].reshape(group_size, shard_count, own_rows, VDIM)
        partial_value = jnp.einsum("hqst,hstv->hqsv", to_bf16_kept(cached_exp), cached_values)
        partial_value = partial_value + jnp.einsum("hqst,hstv->hqsv", to_bf16_kept(new_exp), new_values)
        top = jnp.max(block_max, axis=-1)
        factor = jnp.exp(block_max - top[..., None])
        numer = jnp.sum(factor[..., None] * partial_value, axis=2)
        denom = jnp.sum(factor * block_total, axis=2)
        return numer / denom[..., None]

    results = lax.map(one_group, jnp.arange(H // group_size, dtype=jnp.int32))
    results = results.reshape(H, total_rows, VDIM).transpose(1, 0, 2)
    return results.reshape(total_rows, H * VDIM).astype(jnp.bfloat16)
```

```python
import functools

import jax
import jax.numpy as jnp
from jax import lax
from jax.experimental import pallas as pl
from jax.experimental.pallas import tpu as pltpu
from jax.sharding import PartitionSpec as P

LATENT = 512
ROPE = 64
NOPE = 128
VDIM = 128
HEADS = 16
ROWS = 16
BLOCK = 768
LANES = 128
WIDE = LATENT + LANES
PACKED = HEADS * VDIM + LANES
HIDDEN = -1e30
EXP2_SCALE = (NOPE + ROPE) ** (-0.5) * 1.4426950408889634

CTX = [(z, x, c) for z in range(4) for x in range(4) for c in range(2)]


def ctx_number(z, x, c):
    return (z % 4) * 8 + (x % 4) * 2 + c % 2


def shift_z(k):
    return [(ctx_number(z, x, c), ctx_number(z + k, x, c)) for z, x, c in CTX]


def shift_x(k):
    return [(ctx_number(z, x, c), ctx_number(z, x + k, c)) for z, x, c in CTX]


SWAP_CORE = [(i, i ^ 1) for i in range(32)]
SWAP_ZL = [(i, i ^ 4) for i in range(8)]


def shift_y(k):
    return [(i, (i // 4) * 4 + (i + k) % 4) for i in range(8)]


def split3(value):
    high = value.astype(jnp.bfloat16).astype(jnp.float32)
    rest = value - high
    middle = rest.astype(jnp.bfloat16).astype(jnp.float32)
    low = (rest - middle).astype(jnp.bfloat16).astype(jnp.float32)
    return high, middle, low


def attend_kernel(q0, q1, q2a, q2b, q3, extra, kv_own, kv_far, tail_own, tail_far,
                  out0, out1, out2a, out2b, out3, stats):
    step = pl.program_id(0)
    outs = (out0, out1, out2a, out2b, out3)
    bounds = (0, 64, 128, 160, 192, 256)
    lane = lax.broadcasted_iota(jnp.int32, (256, LANES), 1)
    lower = lane < 64
    queries = jnp.concatenate([r[...] for r in (q0, q1, q2a, q2b, q3)], axis=0).astype(jnp.float32)
    part_a = queries[:, 128:256]
    part_b = queries[:, 256:384]
    marks = extra[...].astype(jnp.float32)
    even = jnp.concatenate([queries[:, :128], jnp.where(lower, part_a, marks)], axis=1)
    nope_odd = jnp.where(lower, pltpu.roll(part_a, 64, 1), pltpu.roll(part_b, 64, 1))
    odd = jnp.concatenate([nope_odd, jnp.where(lower, marks, part_b)], axis=1)
    tails = (
        (tail_own[...], tail_far[...]),
        tuple(
            pltpu.roll(t[...].astype(jnp.float32), 64, 1).astype(jnp.bfloat16)
            for t in (tail_own, tail_far)
        ),
    )
    found = stats[...]
    for side, query in ((0, even), (1, odd)):
        query = query.astype(jnp.bfloat16)
        at = side * 256
        tail_a, tail_b = tails[side]
        key_a = jnp.concatenate([kv_own[:, at : at + 128], tail_a], axis=1)
        key_b = jnp.concatenate([kv_far[:, at : at + 128], tail_b], axis=1)
        key_n = jnp.concatenate([key_a[BLOCK:], key_b[BLOCK:]], axis=0)
        value_a = kv_own[:, at + 128 : at + 256]
        value_b = kv_far[:, at + 128 : at + 256]
        value_n = jnp.concatenate([value_a[BLOCK:], value_b[BLOCK:]], axis=0)

        def score(key):
            return lax.dot_general(
                query, key, (((1,), (1,)), ((), ())), preferred_element_type=jnp.float32
            )

        s_a, s_b, s_n = score(key_a[:BLOCK]), score(key_b[:BLOCK]), score(key_n)
        top = jnp.maximum(
            jnp.max(jnp.maximum(s_a, s_b), axis=1, keepdims=True),
            jnp.max(s_n, axis=1, keepdims=True),
        )
        p_a = jnp.exp2((s_a - top) * EXP2_SCALE)
        p_b = jnp.exp2((s_b - top) * EXP2_SCALE)
        p_n = jnp.exp2((s_n - top) * EXP2_SCALE)
        total = jnp.sum(p_a + p_b, axis=1, keepdims=True) + jnp.sum(p_n, axis=1, keepdims=True)
        result = jnp.dot(
            p_a.astype(jnp.bfloat16), value_a[:BLOCK], preferred_element_type=jnp.float32
        )
        result += jnp.dot(
            p_b.astype(jnp.bfloat16), value_b[:BLOCK], preferred_element_type=jnp.float32
        )
        result += jnp.dot(p_n.astype(jnp.bfloat16), value_n, preferred_element_type=jnp.float32)
        result = result.astype(jnp.bfloat16)
        head = step * 2 + side
        column = pl.multiple_of(head * VDIM, VDIM)
        for out, lo, hi in zip(outs, bounds[:-1], bounds[1:]):
            out[:, pl.ds(column, VDIM)] = result[lo:hi]
        for i, part in enumerate(split3(top) + split3(total)):
            found = jnp.where(lane == head + 16 * i, part, found)
    stats[...] = found
    packed = jnp.where(lane < 96, found, 0.0).astype(jnp.bfloat16)
    for out, lo, hi in zip(outs, bounds[:-1], bounds[1:]):
        out[:, HEADS * VDIM :] = packed[lo:hi]


def attend(chunks, extra, kv_own, kv_far, wide_own, wide_far):
    count = BLOCK + ROWS

    def query_spec(a):
        return pl.BlockSpec((a.shape[0], 384), lambda i: (0, i))

    tail_spec = pl.BlockSpec((count, LANES), lambda i: (0, LATENT // LANES))
    return pl.pallas_call(
        attend_kernel,
        grid=(HEADS // 2,),
        out_shape=[jax.ShapeDtypeStruct((a.shape[0], PACKED), jnp.bfloat16) for a in chunks],
        in_specs=[query_spec(a) for a in chunks]
        + [
            pl.BlockSpec((256, LANES), lambda i: (0, 0)),
            pl.BlockSpec((count, 512), lambda i: (0, i)),
            pl.BlockSpec((count, 512), lambda i: (0, i)),
            tail_spec,
            tail_spec,
        ],
        out_specs=[pl.BlockSpec((a.shape[0], PACKED), lambda i: (0, 0)) for a in chunks],
        scratch_shapes=[pltpu.VMEM((256, LANES), jnp.float32)],
        compiler_params=pltpu.CompilerParams(vmem_limit_bytes=56 * 1024 * 1024),
    )(*chunks, extra, kv_own, kv_far, wide_own, wide_far)


def merge(refs, spans):
    tops, totals = [], []
    for ref, (lo, hi) in zip(refs, spans):
        raw = ref[lo:hi, HEADS * VDIM :].astype(jnp.float32)
        joined = raw + pltpu.roll(raw, 112, 1) + pltpu.roll(raw, 96, 1)
        tops.append(joined)
        totals.append(pltpu.roll(joined, 80, 1))
    top = functools.reduce(jnp.maximum, tops)
    factors = [jnp.exp2((t - top) * EXP2_SCALE) for t in tops]
    total = functools.reduce(jnp.add, [f * t for f, t in zip(factors, totals)])
    values = []
    for head in range(HEADS):
        at = head * VDIM
        values.append(
            functools.reduce(
                jnp.add,
                [
                    f[:, head : head + 1] * ref[lo:hi, at : at + VDIM].astype(jnp.float32)
                    for f, ref, (lo, hi) in zip(factors, refs, spans)
                ],
            )
        )
    return values, top, total


def pack_stats(top, total):
    lane = lax.broadcasted_iota(jnp.int32, top.shape, 1)
    packed = jnp.zeros_like(top)
    for i, part in enumerate(split3(top) + split3(total)):
        here = (lane >= 16 * i) & (lane < 16 * i + 16)
        packed = jnp.where(here, pltpu.roll(part, 16 * i, 1) if i else part, packed)
    return packed.astype(jnp.bfloat16)


def store_merged(out, rows, merged):
    values, top, total = merged
    for head, value in enumerate(values):
        out[rows, head * VDIM : (head + 1) * VDIM] = value.astype(jnp.bfloat16)
    out[rows, HEADS * VDIM :] = pack_stats(top, total)


def first_merge_kernel(own1, own3, from_left, from_right, out1, out3):
    store_merged(out1, slice(0, 32), merge([own1, from_left], [(0, 32), (0, 32)]))
    out1[32:64] = own1[32:64]
    out3[0:32] = own3[0:32]
    store_merged(out3, slice(32, 64), merge([own3, from_right], [(32, 64), (0, 32)]))


def second_merge_kernel(own0, from_left, from_right, *outs):
    refs = [own0, from_left, from_right]
    for i, out in enumerate(outs):
        span = (i * ROWS, (i + 1) * ROWS)
        store_merged(out, slice(0, ROWS), merge(refs, [span] * 3))


def last_merge_kernel(a, b, c, d, out):
    values, top, total = merge([a, b, c, d], [(0, ROWS)] * 4)
    for head, value in enumerate(values):
        out[:, head * VDIM : (head + 1) * VDIM] = (value / total[:, head : head + 1]).astype(
            jnp.bfloat16
        )


def call(kernel, shapes, *args):
    return pl.pallas_call(
        kernel,
        out_shape=shapes,
        compiler_params=pltpu.CompilerParams(vmem_limit_bytes=32 * 1024 * 1024),
    )(*args)


def packed_shape(rows):
    return jax.ShapeDtypeStruct((rows, PACKED), jnp.bfloat16)


def shards(queries, cache, cache_len, new_latents, prefix_len, latent_up):
    bf16 = jnp.bfloat16
    me = lax.axis_index("ctx")
    my_z, my_x, my_core = me // 8, (me // 2) % 4, me % 2

    with jax.named_scope("gather_queries_z"):
        from_z = [queries] + [lax.ppermute(queries, "ctx", shift_z(-k)) for k in (1, 2, 3)]
        chunk0 = jnp.concatenate(from_z, axis=0)
    with jax.named_scope("mark_cache"):
        place = lax.axis_index("head") * cache.shape[0] + jnp.arange(cache.shape[0], dtype=jnp.int32)
        hidden = jnp.where(place < cache_len[0], 0.0, HIDDEN).astype(bf16)
        wide = jnp.concatenate(
            [cache, hidden[:, None], jnp.zeros((cache.shape[0], 63), bf16)], axis=1
        )
        mark = jnp.arange(64, dtype=jnp.int32)[None, :]
        new_row = jnp.arange(ROWS, dtype=jnp.int32)[:, None]
        new_wide = jnp.concatenate(
            [new_latents, (mark == 1 + my_core * ROWS + new_row).astype(bf16)], axis=1
        )
    with jax.named_scope("gather_cache"):
        pair = jnp.concatenate([wide, lax.ppermute(wide, "head", SWAP_ZL)], axis=0)
        up = lax.ppermute(pair, "head", shift_y(-1))
        down = lax.ppermute(pair, "head", shift_y(1))
        up2 = lax.ppermute(up[:96], "head", shift_y(-1))
        down2 = lax.ppermute(down[96:], "head", shift_y(1))
        own = jnp.concatenate([pair, up, down, up2, down2, new_wide], axis=0)
    with jax.named_scope("swap_cores"):
        far = lax.ppermute(own, "ctx", SWAP_CORE)
    with jax.named_scope("gather_queries_x"):
        chunk1 = lax.ppermute(chunk0, "ctx", shift_x(-1))
        chunk3 = lax.ppermute(chunk0, "ctx", shift_x(1))
        chunk2a = lax.ppermute(chunk1[:32], "ctx", shift_x(-1))
        chunk2b = lax.ppermute(chunk3[32:], "ctx", shift_x(1))
    with jax.named_scope("marks"):
        row = jnp.arange(256, dtype=jnp.int32)[:, None]
        row_z = (my_z + (row // 16) % 4) % 4
        row_x = (my_x + row // 64) % 4
        query_index = ((row_z * 8 + row_x * 2 + my_core) * ROWS) + row % 16
        lane = jnp.arange(LANES, dtype=jnp.int32)[None, :] % 64
        new_at = lane - 1
        new_index = ((my_z * 8 + my_x * 2 + new_at // 16) * ROWS) + new_at % 16
        visible = (new_index <= query_index) | (new_index < prefix_len[0])
        extra = jnp.where(
            lane == 0, 1.0, jnp.where((lane > 32) | visible, 0.0, HIDDEN)
        ).astype(bf16)

    def lift(source):
        return jnp.dot(source[:, :LATENT], latent_up, preferred_element_type=jnp.float32).astype(bf16)

    with jax.named_scope("lift"):
        kv_own = lift(own)
        kv_far = lift(far)
    with jax.named_scope("attend"):
        out0, out1, out2a, out2b, out3 = attend(
            [chunk0, chunk1, chunk2a, chunk2b, chunk3], extra, kv_own, kv_far, own, far
        )
    with jax.named_scope("reduce_x"):
        left2 = lax.ppermute(out2a, "ctx", shift_x(1))
        right2 = lax.ppermute(out2b, "ctx", shift_x(-1))
        sum1, sum3 = call(first_merge_kernel, [packed_shape(64)] * 2, out1, out3, left2, right2)
        left1 = lax.ppermute(sum1, "ctx", shift_x(1))
        right1 = lax.ppermute(sum3, "ctx", shift_x(-1))
        parts = call(second_merge_kernel, [packed_shape(ROWS)] * 4, out0, left1, right1)
    with jax.named_scope("reduce_z"):
        arrived = [lax.ppermute(parts[k], "ctx", shift_z(k)) for k in (1, 2, 3)]
        return call(
            last_merge_kernel,
            jax.ShapeDtypeStruct((ROWS, HEADS * VDIM), bf16),
            parts[0],
            *arrived,
        )


def solution(mesh):
    placed = (
        P("ctx", "head"),
        P(("ctx", "head"), None),
        P("ctx"),
        P("ctx", None),
        P(),
        P(None, "head"),
    )
    return jax.shard_map(
        shards, mesh=mesh, in_specs=placed, out_specs=P("ctx", "head"), check_vma=False
    )
```

```python
import functools

import jax
import jax.numpy as jnp
from jax import lax
from jax.experimental import pallas as pl
from jax.experimental.pallas import tpu as pltpu
from jax.sharding import PartitionSpec as P

LATENT = 512
ROPE = 64
NOPE = 128
VDIM = 128
HEADS = 16
ROWS = 16
BLOCK = 768
LANES = 128
WIDE = LATENT + LANES
PACKED = HEADS * VDIM + LANES
SPLIT = (0, 64, 128, 160, 192, 256)
CHUNKS = (
    [(0, 0, 256)],
    [(0, 256, 512)],
    [(0, 512, 768)],
    [(1, 0, 256)],
    [(1, 256, 512)],
    [(1, 512, 768)],
    [(0, 768, 784), (1, 768, 784)],
)
LIFTS = (slice(0, 256), slice(256, 512), slice(512, 784))
HIDDEN = -1e30
EXP2_SCALE = (NOPE + ROPE) ** (-0.5) * 1.4426950408889634

CTX = [(z, x, c) for z in range(4) for x in range(4) for c in range(2)]


def ctx_number(z, x, c):
    return (z % 4) * 8 + (x % 4) * 2 + c % 2


def shift_z(k):
    return [(ctx_number(z, x, c), ctx_number(z + k, x, c)) for z, x, c in CTX]


def shift_x(k):
    return [(ctx_number(z, x, c), ctx_number(z, x + k, c)) for z, x, c in CTX]


SWAP_CORE = [(i, i ^ 1) for i in range(32)]
SWAP_ZL = [(i, i ^ 4) for i in range(8)]


def shift_y(k):
    return [(i, (i // 4) * 4 + (i + k) % 4) for i in range(8)]


def split3(value):
    high = value.astype(jnp.bfloat16).astype(jnp.float32)
    rest = value - high
    middle = rest.astype(jnp.bfloat16).astype(jnp.float32)
    low = (rest - middle).astype(jnp.bfloat16).astype(jnp.float32)
    return high, middle, low


def scores_of(keys, query):
    return lax.dot_general(
        keys, query, (((1,), (1,)), ((), ())), preferred_element_type=jnp.float32
    )


def weighted(values, weights):
    return lax.dot_general(
        values, weights, (((0,), (0,)), ((), ())), preferred_element_type=jnp.float32
    )


def fold(array, op):
    return functools.reduce(op, [array[i : i + 8] for i in range(0, array.shape[0], 8)])


def head_queries(refs, extra):
    lower = lax.broadcasted_iota(jnp.int32, (256, LANES), 1) < 64
    pair = jnp.concatenate([r[...] for r in refs], axis=0).astype(jnp.float32)
    a, b = pair[:, 128:256], pair[:, 256:384]
    marks = extra[...].astype(jnp.float32)
    a_turned, b_turned = pltpu.roll(a, 64, 1), pltpu.roll(b, 64, 1)
    even = [pair[:, :128], jnp.where(lower, a, marks)]
    odd = [jnp.where(lower, a_turned, b_turned), jnp.where(lower, b_turned, marks)]
    return [jnp.concatenate(q, axis=1).astype(jnp.bfloat16) for q in (even, odd)]


def attend_kernel(*refs):
    query_refs, extra, sources, lift_ref, kv_own = refs[:5], refs[5], refs[6:8], refs[8], refs[9]
    outs, (stats, score_buf, max_buf, lifted, query_buf, value_buf) = refs[10:15], refs[15:]
    step = pl.program_id(0)
    steps = HEADS // 2
    sizes = [sum(hi - lo for _, lo, hi in chunk) for chunk in CHUNKS]
    spans = [slice(sum(sizes[:i]), sum(sizes[: i + 1])) for i in range(len(sizes))]
    row = lax.broadcasted_iota(jnp.int32, (LANES, 256), 0)

    def tail_of(number):
        return jnp.concatenate([sources[i][a:b, LATENT:] for i, a, b in CHUNKS[number]], axis=0)

    def taken(number, slot, at):
        parts = [
            lifted[slot, a:b, at : at + 128] if i else kv_own[a:b, at : at + 128]
            for i, a, b in CHUNKS[number]
        ]
        return jnp.concatenate(parts, axis=0)

    def lift(rows, slot):
        product = jnp.dot(
            sources[1][rows, :LATENT], lift_ref[...], preferred_element_type=jnp.float32
        )
        lifted[slot, rows] = product.astype(jnp.bfloat16)

    def keep_queries(slot):
        for side, query in enumerate(head_queries(query_refs, extra)):
            query_buf[slot, side] = query

    def finish(top, total, result, head):
        column = pl.multiple_of(head * VDIM, VDIM)
        result = result.T.astype(jnp.bfloat16)
        for out, lo, hi in zip(outs, SPLIT, SPLIT[1:]):
            out[:, pl.ds(column, VDIM)] = result[lo:hi]
        found = stats[...]
        for i, part in enumerate(split3(top) + split3(total)):
            found = jnp.where(row == head + HEADS * i, part, found)
        stats[...] = found

    def phase(side, done_head, slot, lifts):
        done = 1 if side is None else 1 - side
        lifts = list(lifts)
        top = jnp.max(max_buf[done], axis=0, keepdims=True)
        total = jnp.zeros((8, 256), jnp.float32)
        result = jnp.zeros((VDIM, 256), jnp.float32)
        highest = jnp.full((8, 256), -jnp.inf, jnp.float32)
        for number, here in enumerate(spans):
            weights = jnp.exp2((score_buf[done, here] - top) * EXP2_SCALE)
            total += fold(weights, jnp.add)
            weights = weights.astype(jnp.bfloat16)
            if lifts and number % 3 == 0:
                lift(lifts.pop(0), 1 - slot)
            values = taken(number, slot, 128) if side == 1 else value_buf[here]
            result += weighted(values, weights)
            if side is not None:
                keys = jnp.concatenate([taken(number, slot, side * 256), tail_of(number)], axis=1)
                scores = scores_of(keys, query_buf[slot, side])
                score_buf[side, here] = scores
                highest = jnp.maximum(highest, fold(scores, jnp.maximum))
                if side == 1:
                    value_buf[here] = taken(number, slot, 384)
        for rows in lifts:
            lift(rows, 1 - slot)
        if side is not None:
            max_buf[side] = highest
        finish(top, jnp.sum(total, axis=0, keepdims=True), result, done_head)

    @pl.when(step == 0)
    def _():
        keep_queries(0)
        for rows in LIFTS:
            lift(rows, 0)

    for parity in range(2):

        @pl.when((step > 0) & (step < steps) & (step % 2 == parity))
        def _():
            phase(0, jnp.maximum(step * 2 - 3, 0), 1 - parity, LIFTS[:2])
            phase(1, step * 2 - 2, 1 - parity, LIFTS[2:])
            keep_queries(parity)

    @pl.when(step == steps)
    def _():
        slot = (steps - 1) % 2
        phase(0, HEADS - 3, slot, ())
        phase(1, HEADS - 2, slot, ())
        phase(None, HEADS - 1, slot, ())
        packed = jnp.where(row < 6 * HEADS, stats[...], 0.0).T.astype(jnp.bfloat16)
        for out, lo, hi in zip(outs, SPLIT, SPLIT[1:]):
            out[:, HEADS * VDIM :] = packed[lo:hi]


def attend(chunks, extra, sources, latent_up, kv_own):
    steps = HEADS // 2

    def pair(i):
        return 0, jnp.minimum(i, steps - 1)

    def pair_before(i):
        return 0, jnp.maximum(i - 1, 0)

    def whole(i):
        return 0, 0

    total = sum(source.shape[0] for source in sources)
    return pl.pallas_call(
        attend_kernel,
        grid=(steps + 1,),
        out_shape=[packed_shape(a.shape[0]) for a in chunks],
        in_specs=[pl.BlockSpec((a.shape[0], 384), pair) for a in chunks]
        + [pl.BlockSpec(a.shape, whole) for a in (extra, *sources)]
        + [pl.BlockSpec((LATENT, 512), pair)]
        + [pl.BlockSpec((kv_own.shape[0], 512), pair_before)],
        out_specs=[pl.BlockSpec((a.shape[0], PACKED), whole) for a in chunks],
        scratch_shapes=[
            pltpu.VMEM((LANES, 256), jnp.float32),
            pltpu.VMEM((2, total, 256), jnp.float32),
            pltpu.VMEM((2, 8, 256), jnp.float32),
            pltpu.VMEM((2, total - kv_own.shape[0], 512), jnp.bfloat16),
            pltpu.VMEM((2, 2, 256, 256), jnp.bfloat16),
            pltpu.VMEM((total, VDIM), jnp.bfloat16),
        ],
        name="attend",
        compiler_params=pltpu.CompilerParams(vmem_limit_bytes=48 * 1024 * 1024),
    )(*chunks, extra, *sources, latent_up, kv_own)


def merge(refs, spans):
    tops, totals = [], []
    for ref, (lo, hi) in zip(refs, spans):
        raw = ref[lo:hi, HEADS * VDIM :].astype(jnp.float32)
        joined = raw + pltpu.roll(raw, 112, 1) + pltpu.roll(raw, 96, 1)
        tops.append(joined)
        totals.append(pltpu.roll(joined, 80, 1))
    top = functools.reduce(jnp.maximum, tops)
    factors = [jnp.exp2((t - top) * EXP2_SCALE) for t in tops]
    total = functools.reduce(jnp.add, [f * t for f, t in zip(factors, totals)])
    values = []
    for head in range(HEADS):
        at = head * VDIM
        values.append(
            functools.reduce(
                jnp.add,
                [
                    f[:, head : head + 1] * ref[lo:hi, at : at + VDIM].astype(jnp.float32)
                    for f, ref, (lo, hi) in zip(factors, refs, spans)
                ],
            )
        )
    return values, top, total


def pack_stats(top, total):
    lane = lax.broadcasted_iota(jnp.int32, top.shape, 1)
    packed = jnp.zeros_like(top)
    for i, part in enumerate(split3(top) + split3(total)):
        here = (lane >= 16 * i) & (lane < 16 * i + 16)
        packed = jnp.where(here, pltpu.roll(part, 16 * i, 1) if i else part, packed)
    return packed.astype(jnp.bfloat16)


def store_merged(out, rows, merged):
    values, top, total = merged
    for head, value in enumerate(values):
        out[rows, head * VDIM : (head + 1) * VDIM] = value.astype(jnp.bfloat16)
    out[rows, HEADS * VDIM :] = pack_stats(top, total)


def first_merge_kernel(own1, own3, from_left, from_right, out1, out3):
    store_merged(out1, slice(0, 32), merge([own1, from_left], [(0, 32), (0, 32)]))
    out1[32:64] = own1[32:64]
    out3[0:32] = own3[0:32]
    store_merged(out3, slice(32, 64), merge([own3, from_right], [(32, 64), (0, 32)]))


def second_merge_kernel(own0, from_left, from_right, *outs):
    refs = [own0, from_left, from_right]
    for i, out in enumerate(outs):
        span = (i * ROWS, (i + 1) * ROWS)
        store_merged(out, slice(0, ROWS), merge(refs, [span] * 3))


def last_merge_kernel(a, b, c, d, out):
    values, top, total = merge([a, b, c, d], [(0, ROWS)] * 4)
    for head, value in enumerate(values):
        out[:, head * VDIM : (head + 1) * VDIM] = (value / total[:, head : head + 1]).astype(
            jnp.bfloat16
        )


def call(kernel, shapes, *args):
    return pl.pallas_call(
        kernel,
        out_shape=shapes,
        compiler_params=pltpu.CompilerParams(vmem_limit_bytes=32 * 1024 * 1024),
    )(*args)


def packed_shape(rows):
    return jax.ShapeDtypeStruct((rows, PACKED), jnp.bfloat16)


def shards(queries, cache, cache_len, new_latents, prefix_len, latent_up):
    bf16 = jnp.bfloat16
    me = lax.axis_index("ctx")
    my_z, my_x, my_core = me // 8, (me // 2) % 4, me % 2

    with jax.named_scope("mark_cache"):
        place = lax.axis_index("head") * cache.shape[0] + jnp.arange(cache.shape[0], dtype=jnp.int32)
        hidden = jnp.where(place < cache_len[0], 0.0, HIDDEN).astype(bf16)
        wide = jnp.concatenate(
            [cache, hidden[:, None], jnp.zeros((cache.shape[0], 63), bf16)], axis=1
        )
        mark = jnp.arange(64, dtype=jnp.int32)[None, :]
        new_row = jnp.arange(ROWS, dtype=jnp.int32)[:, None]
        new_wide = jnp.concatenate(
            [new_latents, (mark == 1 + my_core * ROWS + new_row).astype(bf16)], axis=1
        )
    with jax.named_scope("first_hop"):
        above = lax.ppermute(queries, "ctx", shift_z(-1))
        below = lax.ppermute(queries, "ctx", shift_z(1))
        pair = jnp.concatenate([wide, lax.ppermute(wide, "head", SWAP_ZL)], axis=0)
    pair, above, below = lax.optimization_barrier((pair, above, below))
    with jax.named_scope("second_hop"):
        half = queries.shape[1] // 2
        across = [
            lax.ppermute(above[:, :half], "ctx", shift_z(-1)),
            lax.ppermute(below[:, half:], "ctx", shift_z(1)),
        ]
        chunk0 = jnp.concatenate(
            [queries, above, jnp.concatenate(across, axis=1), below], axis=0
        )
        up = lax.ppermute(pair, "head", shift_y(-1))
        down = lax.ppermute(pair, "head", shift_y(1))
    with jax.named_scope("third_hop"):
        chunk1 = lax.ppermute(chunk0, "ctx", shift_x(-1))
        chunk3 = lax.ppermute(chunk0, "ctx", shift_x(1))
        up2 = lax.ppermute(up[:96], "head", shift_y(-1))
        down2 = lax.ppermute(down[96:], "head", shift_y(1))
        own = jnp.concatenate([pair, up, down, up2, down2, new_wide], axis=0)
    chunk1, chunk3, *_ = lax.optimization_barrier((chunk1, chunk3, up2, down2))
    with jax.named_scope("fourth_hop"):
        far = lax.ppermute(own, "ctx", SWAP_CORE)
        chunk2a = lax.ppermute(chunk1[:32], "ctx", shift_x(-1))
        chunk2b = lax.ppermute(chunk3[32:], "ctx", shift_x(1))
    with jax.named_scope("marks"):
        row = jnp.arange(256, dtype=jnp.int32)[:, None]
        row_z = (my_z + (row // 16) % 4) % 4
        row_x = (my_x + row // 64) % 4
        query_index = ((row_z * 8 + row_x * 2 + my_core) * ROWS) + row % 16
        lane = jnp.arange(LANES, dtype=jnp.int32)[None, :] % 64
        new_at = lane - 1
        new_index = ((my_z * 8 + my_x * 2 + new_at // 16) * ROWS) + new_at % 16
        visible = (new_index <= query_index) | (new_index < prefix_len[0])
        extra = jnp.where(
            lane == 0, 1.0, jnp.where((lane > 32) | visible, 0.0, HIDDEN)
        ).astype(bf16)

    with jax.named_scope("lift_own"):
        kv_own = jnp.dot(own[:, :LATENT], latent_up, preferred_element_type=jnp.float32).astype(bf16)
    sources = [own, far]
    chunks = [chunk0, chunk1, chunk2a, chunk2b, chunk3]
    with jax.named_scope("attend"):
        out0, out1, out2a, out2b, out3 = attend(
            chunks, extra, sources, latent_up, kv_own
        )
    with jax.named_scope("reduce_x"):
        left2 = lax.ppermute(out2a, "ctx", shift_x(1))
        right2 = lax.ppermute(out2b, "ctx", shift_x(-1))
        sum1, sum3 = call(first_merge_kernel, [packed_shape(64)] * 2, out1, out3, left2, right2)
        left1 = lax.ppermute(sum1, "ctx", shift_x(1))
        right1 = lax.ppermute(sum3, "ctx", shift_x(-1))
        parts = call(second_merge_kernel, [packed_shape(ROWS)] * 4, out0, left1, right1)
    with jax.named_scope("reduce_z"):
        arrived = [lax.ppermute(parts[k], "ctx", shift_z(k)) for k in (1, 2, 3)]
        return call(
            last_merge_kernel,
            jax.ShapeDtypeStruct((ROWS, HEADS * VDIM), bf16),
            parts[0],
            *arrived,
        )


def solution(mesh):
    placed = (
        P("ctx", "head"),
        P(("ctx", "head"), None),
        P("ctx"),
        P("ctx", None),
        P(),
        P(None, "head"),
    )
    return jax.shard_map(
        shards, mesh=mesh, in_specs=placed, out_specs=P("ctx", "head"), check_vma=False
    )
```

```python
import functools

import jax
import jax.numpy as jnp
from jax import lax
from jax.experimental import pallas as pl
from jax.experimental.pallas import tpu as pltpu
from jax.sharding import PartitionSpec as P

LATENT = 512
ROPE = 64
NOPE = 128
VDIM = 128
HEADS = 16
ROWS = 16
BLOCK = 768
LANES = 128
WIDE = LATENT + LANES
PACKED = HEADS * VDIM + LANES
SPLIT = (0, 64, 96, 128, 160, 192, 224, 256)
CHUNKS = (
    [(0, 0, 256)],
    [(0, 256, 512)],
    [(0, 512, 768)],
    [(1, 0, 256)],
    [(1, 256, 512)],
    [(1, 512, 768)],
    [(0, 768, 784), (1, 768, 784)],
)
LIFTS = (slice(0, 256), slice(256, 512), slice(512, 784))
HIDDEN = -1e30
EXP2_SCALE = (NOPE + ROPE) ** (-0.5) * 1.4426950408889634

CTX = [(z, x, c) for z in range(4) for x in range(4) for c in range(2)]


def ctx_number(z, x, c):
    return (z % 4) * 8 + (x % 4) * 2 + c % 2


def shift_z(k):
    return [(ctx_number(z, x, c), ctx_number(z + k, x, c)) for z, x, c in CTX]


def shift_x(k):
    return [(ctx_number(z, x, c), ctx_number(z, x + k, c)) for z, x, c in CTX]


SWAP_CORE = [(i, i ^ 1) for i in range(32)]
SWAP_ZL = [(i, i ^ 4) for i in range(8)]


def shift_y(k):
    return [(i, (i // 4) * 4 + (i + k) % 4) for i in range(8)]


def split3(value):
    high = value.astype(jnp.bfloat16).astype(jnp.float32)
    rest = value - high
    middle = rest.astype(jnp.bfloat16).astype(jnp.float32)
    low = (rest - middle).astype(jnp.bfloat16).astype(jnp.float32)
    return high, middle, low


def scores_of(keys, query):
    return lax.dot_general(
        keys, query, (((1,), (1,)), ((), ())), preferred_element_type=jnp.float32
    )


def weighted(values, weights):
    return lax.dot_general(
        values, weights, (((0,), (0,)), ((), ())), preferred_element_type=jnp.float32
    )


def fold(array, op):
    return functools.reduce(op, [array[i : i + 8] for i in range(0, array.shape[0], 8)])


def head_queries(refs, extra):
    lower = lax.broadcasted_iota(jnp.int32, (256, LANES), 1) < 64
    pair = jnp.concatenate([r[...] for r in refs], axis=0).astype(jnp.float32)
    a, b = pair[:, 128:256], pair[:, 256:384]
    marks = extra[...].astype(jnp.float32)
    a_turned, b_turned = pltpu.roll(a, 64, 1), pltpu.roll(b, 64, 1)
    even = [pair[:, :128], jnp.where(lower, a, marks)]
    odd = [jnp.where(lower, a_turned, b_turned), jnp.where(lower, b_turned, marks)]
    return [jnp.concatenate(q, axis=1).astype(jnp.bfloat16) for q in (even, odd)]


def attend_kernel(*refs):
    query_refs, extra, sources, lift_ref, kv_own = refs[:5], refs[5], refs[6:8], refs[8], refs[9]
    outs, (stats, score_buf, max_buf, lifted, query_buf, value_buf) = refs[10:17], refs[17:]
    step = pl.program_id(0)
    steps = HEADS // 2
    sizes = [sum(hi - lo for _, lo, hi in chunk) for chunk in CHUNKS]
    spans = [slice(sum(sizes[:i]), sum(sizes[: i + 1])) for i in range(len(sizes))]
    row = lax.broadcasted_iota(jnp.int32, (LANES, 256), 0)

    def tail_of(number):
        return jnp.concatenate([sources[i][a:b, LATENT:] for i, a, b in CHUNKS[number]], axis=0)

    def taken(number, slot, at):
        parts = [
            lifted[slot, a:b, at : at + 128] if i else kv_own[a:b, at : at + 128]
            for i, a, b in CHUNKS[number]
        ]
        return jnp.concatenate(parts, axis=0)

    def lift(rows, slot):
        product = jnp.dot(
            sources[1][rows, :LATENT], lift_ref[...], preferred_element_type=jnp.float32
        )
        lifted[slot, rows] = product.astype(jnp.bfloat16)

    def keep_queries(slot):
        for side, query in enumerate(head_queries(query_refs, extra)):
            query_buf[slot, side] = query

    def finish(top, total, result, head):
        column = pl.multiple_of(head * VDIM, VDIM)
        result = result.T.astype(jnp.bfloat16)
        for out, lo, hi in zip(outs, SPLIT, SPLIT[1:]):
            out[:, pl.ds(column, VDIM)] = result[lo:hi]
        found = stats[...]
        for i, part in enumerate(split3(top) + split3(total)):
            found = jnp.where(row == head + HEADS * i, part, found)
        stats[...] = found

    def phase(side, done_head, slot, lifts):
        done = 1 if side is None else 1 - side
        lifts = list(lifts)
        top = jnp.max(max_buf[done], axis=0, keepdims=True)
        total = jnp.zeros((8, 256), jnp.float32)
        result = jnp.zeros((VDIM, 256), jnp.float32)
        highest = jnp.full((8, 256), -jnp.inf, jnp.float32)
        for number, here in enumerate(spans):
            weights = jnp.exp2((score_buf[done, here] - top) * EXP2_SCALE)
            total += fold(weights, jnp.add)
            weights = weights.astype(jnp.bfloat16)
            if lifts and number % 3 == 0:
                lift(lifts.pop(0), 1 - slot)
            values = taken(number, slot, 128) if side == 1 else value_buf[here]
            result += weighted(values, weights)
            if side is not None:
                keys = jnp.concatenate([taken(number, slot, side * 256), tail_of(number)], axis=1)
                scores = scores_of(keys, query_buf[slot, side])
                score_buf[side, here] = scores
                highest = jnp.maximum(highest, fold(scores, jnp.maximum))
                if side == 1:
                    value_buf[here] = taken(number, slot, 384)
        for rows in lifts:
            lift(rows, 1 - slot)
        if side is not None:
            max_buf[side] = highest
        finish(top, jnp.sum(total, axis=0, keepdims=True), result, done_head)

    @pl.when(step == 0)
    def _():
        keep_queries(0)
        for rows in LIFTS:
            lift(rows, 0)

    for parity in range(2):

        @pl.when((step > 0) & (step < steps) & (step % 2 == parity))
        def _():
            phase(0, jnp.maximum(step * 2 - 3, 0), 1 - parity, LIFTS[:2])
            phase(1, step * 2 - 2, 1 - parity, LIFTS[2:])
            keep_queries(parity)

    @pl.when(step == steps)
    def _():
        slot = (steps - 1) % 2
        phase(0, HEADS - 3, slot, ())
        phase(1, HEADS - 2, slot, ())
        phase(None, HEADS - 1, slot, ())
        packed = jnp.where(row < 6 * HEADS, stats[...], 0.0).T.astype(jnp.bfloat16)
        for out, lo, hi in zip(outs, SPLIT, SPLIT[1:]):
            out[:, HEADS * VDIM :] = packed[lo:hi]


def attend(chunks, extra, sources, latent_up, kv_own):
    steps = HEADS // 2

    def pair(i):
        return 0, jnp.minimum(i, steps - 1)

    def pair_before(i):
        return 0, jnp.maximum(i - 1, 0)

    def whole(i):
        return 0, 0

    total = sum(source.shape[0] for source in sources)
    return pl.pallas_call(
        attend_kernel,
        grid=(steps + 1,),
        out_shape=[packed_shape(hi - lo) for lo, hi in zip(SPLIT, SPLIT[1:])],
        in_specs=[pl.BlockSpec((a.shape[0], 384), pair) for a in chunks]
        + [pl.BlockSpec(a.shape, whole) for a in (extra, *sources)]
        + [pl.BlockSpec((LATENT, 512), pair)]
        + [pl.BlockSpec((kv_own.shape[0], 512), pair_before)],
        out_specs=[pl.BlockSpec((hi - lo, PACKED), whole) for lo, hi in zip(SPLIT, SPLIT[1:])],
        scratch_shapes=[
            pltpu.VMEM((LANES, 256), jnp.float32),
            pltpu.VMEM((2, total, 256), jnp.float32),
            pltpu.VMEM((2, 8, 256), jnp.float32),
            pltpu.VMEM((2, total - kv_own.shape[0], 512), jnp.bfloat16),
            pltpu.VMEM((2, 2, 256, 256), jnp.bfloat16),
            pltpu.VMEM((total, VDIM), jnp.bfloat16),
        ],
        name="attend",
        compiler_params=pltpu.CompilerParams(vmem_limit_bytes=48 * 1024 * 1024),
    )(*chunks, extra, *sources, latent_up, kv_own)


def merge(refs, spans):
    tops, totals = [], []
    for ref, (lo, hi) in zip(refs, spans):
        raw = ref[lo:hi, HEADS * VDIM :].astype(jnp.float32)
        joined = raw + pltpu.roll(raw, 112, 1) + pltpu.roll(raw, 96, 1)
        tops.append(joined)
        totals.append(pltpu.roll(joined, 80, 1))
    top = functools.reduce(jnp.maximum, tops)
    factors = [jnp.exp2((t - top) * EXP2_SCALE) for t in tops]
    total = functools.reduce(jnp.add, [f * t for f, t in zip(factors, totals)])
    values = []
    for head in range(HEADS):
        at = head * VDIM
        values.append(
            functools.reduce(
                jnp.add,
                [
                    f[:, head : head + 1] * ref[lo:hi, at : at + VDIM].astype(jnp.float32)
                    for f, ref, (lo, hi) in zip(factors, refs, spans)
                ],
            )
        )
    return values, top, total


def pack_stats(top, total):
    lane = lax.broadcasted_iota(jnp.int32, top.shape, 1)
    packed = jnp.zeros_like(top)
    for i, part in enumerate(split3(top) + split3(total)):
        here = (lane >= 16 * i) & (lane < 16 * i + 16)
        packed = jnp.where(here, pltpu.roll(part, 16 * i, 1) if i else part, packed)
    return packed.astype(jnp.bfloat16)


def store_merged(out, rows, merged):
    values, top, total = merged
    for head, value in enumerate(values):
        out[rows, head * VDIM : (head + 1) * VDIM] = value.astype(jnp.bfloat16)
    out[rows, HEADS * VDIM :] = pack_stats(top, total)


def first_merge_kernel(own1, own3, from_left, from_right, out1, out3):
    for out, own, other in ((out1, own1, from_left), (out3, own3, from_right)):
        store_merged(out, slice(0, 32), merge([own, other], [(0, 32)] * 2))


def second_merge_kernel(own, left_a, left_b, right_a, right_b, *outs):
    for i, out in enumerate(outs):
        lo, at = i * ROWS, (i % 2) * ROWS
        refs = [own, left_a, right_a] if i < 2 else [own, left_b, right_b]
        spans = [(lo, lo + ROWS)] + [(at, at + ROWS)] * 2
        store_merged(out, slice(0, ROWS), merge(refs, spans))


def last_merge_kernel(a, b, c, d, out):
    values, top, total = merge([a, b, c, d], [(0, ROWS)] * 4)
    for head, value in enumerate(values):
        out[:, head * VDIM : (head + 1) * VDIM] = (value / total[:, head : head + 1]).astype(
            jnp.bfloat16
        )


def call(kernel, shapes, *args):
    return pl.pallas_call(
        kernel,
        out_shape=shapes,
        compiler_params=pltpu.CompilerParams(vmem_limit_bytes=32 * 1024 * 1024),
    )(*args)


def packed_shape(rows):
    return jax.ShapeDtypeStruct((rows, PACKED), jnp.bfloat16)


def shards(queries, cache, cache_len, new_latents, prefix_len, latent_up):
    bf16 = jnp.bfloat16
    me = lax.axis_index("ctx")
    my_z, my_x, my_core = me // 8, (me // 2) % 4, me % 2

    with jax.named_scope("mark_new"):
        mark = jnp.arange(64, dtype=jnp.int32)[None, :]
        new_row = jnp.arange(ROWS, dtype=jnp.int32)[:, None]
        new_wide = jnp.concatenate(
            [new_latents, (mark == 1 + my_core * ROWS + new_row).astype(bf16)], axis=1
        )
    with jax.named_scope("first_hop"):
        above = lax.ppermute(queries, "ctx", shift_z(-1))
        below = lax.ppermute(queries, "ctx", shift_z(1))
        up = lax.ppermute(cache, "head", shift_y(-1))
        down = lax.ppermute(cache, "head", shift_y(1))
    above, below, up, down = lax.optimization_barrier((above, below, up, down))
    with jax.named_scope("second_hop"):
        half = queries.shape[1] // 2
        across = [
            lax.ppermute(above[:, :half], "ctx", shift_z(-1)),
            lax.ppermute(below[:, half:], "ctx", shift_z(1)),
        ]
        chunk0 = jnp.concatenate(
            [queries, above, jnp.concatenate(across, axis=1), below], axis=0
        )
        up2 = lax.ppermute(up[:48], "head", shift_y(-1))
        down2 = lax.ppermute(down[48:], "head", shift_y(1))
        here = jnp.concatenate([cache, up, down, up2, down2], axis=0)
    chunk0, here = lax.optimization_barrier((chunk0, here))
    with jax.named_scope("third_hop"):
        chunk1 = lax.ppermute(chunk0, "ctx", shift_x(-1))
        chunk3 = lax.ppermute(chunk0, "ctx", shift_x(1))
        there = lax.ppermute(here, "head", SWAP_ZL)
    with jax.named_scope("mark_cache"):
        rows, head = cache.shape[0], lax.axis_index("head")
        index = jnp.arange(8 * rows, dtype=jnp.int32)
        turn = (index // rows) % 4
        y_from = (head + jnp.where(turn < 2, turn, 5 - turn)) % 4
        zl_from = (head // 4 + index // (4 * rows)) % 2
        place = (zl_from * 4 + y_from) * rows + index % rows
        hidden = jnp.where(place < cache_len[0], 0.0, HIDDEN).astype(bf16)
        hidden = jnp.where(jnp.arange(64)[None, :] == 0, hidden[:, None], 0.0).astype(bf16)
        block = jnp.concatenate([jnp.concatenate([here, there], axis=0), hidden], axis=1)
        own = jnp.concatenate([block, new_wide], axis=0)
    with jax.named_scope("fourth_hop"):
        far = lax.ppermute(own, "ctx", SWAP_CORE)
        chunk2a = lax.ppermute(chunk1[:32], "ctx", shift_x(-1))
        chunk2b = lax.ppermute(chunk3[32:], "ctx", shift_x(1))
    with jax.named_scope("marks"):
        row = jnp.arange(256, dtype=jnp.int32)[:, None]
        row_z = (my_z + (row // 16) % 4) % 4
        row_x = (my_x + row // 64) % 4
        query_index = ((row_z * 8 + row_x * 2 + my_core) * ROWS) + row % 16
        lane = jnp.arange(LANES, dtype=jnp.int32)[None, :] % 64
        new_at = lane - 1
        new_index = ((my_z * 8 + my_x * 2 + new_at // 16) * ROWS) + new_at % 16
        visible = (new_index <= query_index) | (new_index < prefix_len[0])
        extra = jnp.where(
            lane == 0, 1.0, jnp.where((lane > 32) | visible, 0.0, HIDDEN)
        ).astype(bf16)

    with jax.named_scope("lift_own"):
        kv_own = jnp.dot(own[:, :LATENT], latent_up, preferred_element_type=jnp.float32).astype(bf16)
    sources = [own, far]
    chunks = [chunk0, chunk1, chunk2a, chunk2b, chunk3]
    with jax.named_scope("attend"):
        out0, out1a, out1b, out2a, out2b, out3a, out3b = attend(
            chunks, extra, sources, latent_up, kv_own
        )
    with jax.named_scope("reduce_x"):
        left2 = lax.ppermute(out2a, "ctx", shift_x(1))
        right2 = lax.ppermute(out2b, "ctx", shift_x(-1))
        left_b = lax.ppermute(out1b, "ctx", shift_x(1))
        right_a = lax.ppermute(out3a, "ctx", shift_x(-1))
        sum1, sum3 = call(first_merge_kernel, [packed_shape(32)] * 2, out1a, out3b, left2, right2)
        left_a = lax.ppermute(sum1, "ctx", shift_x(1))
        right_b = lax.ppermute(sum3, "ctx", shift_x(-1))
        shapes = [packed_shape(ROWS)] * 4
        parts = call(second_merge_kernel, shapes, out0, left_a, left_b, right_a, right_b)
    with jax.named_scope("reduce_z"):
        arrived = [lax.ppermute(parts[k], "ctx", shift_z(k)) for k in (1, 2, 3)]
        return call(
            last_merge_kernel,
            jax.ShapeDtypeStruct((ROWS, HEADS * VDIM), bf16),
            parts[0],
            *arrived,
        )


def solution(mesh):
    placed = (
        P("ctx", "head"),
        P(("ctx", "head"), None),
        P("ctx"),
        P("ctx", None),
        P(),
        P(None, "head"),
    )
    return jax.shard_map(
        shards, mesh=mesh, in_specs=placed, out_specs=P("ctx", "head"), check_vma=False
    )
```

```python
import functools

import jax
import jax.numpy as jnp
from jax import lax
from jax.experimental import pallas as pl
from jax.experimental.pallas import tpu as pltpu
from jax.sharding import PartitionSpec as P

LATENT = 512
ROPE = 64
NOPE = 128
VDIM = 128
HEADS = 16
ROWS = 16
BLOCK = 768
LANES = 128
WIDE = LATENT + LANES
PACKED = HEADS * VDIM + LANES
SPLIT = (0, 64, 96, 128, 160, 192, 224, 256)
CHUNKS = (
    [(0, 0, 512)],
    [(0, 512, 768), (1, 0, 256)],
    [(1, 256, 768)],
    [(0, 768, 784), (1, 768, 784)],
)
LIFTS = (slice(0, 400), slice(400, 784))
HIDDEN = -1e30
EXP2_SCALE = (NOPE + ROPE) ** (-0.5) * 1.4426950408889634

CTX = [(z, x, c) for z in range(4) for x in range(4) for c in range(2)]


def ctx_number(z, x, c):
    return (z % 4) * 8 + (x % 4) * 2 + c % 2


def shift_z(k):
    return [(ctx_number(z, x, c), ctx_number(z + k, x, c)) for z, x, c in CTX]


def shift_x(k):
    return [(ctx_number(z, x, c), ctx_number(z, x + k, c)) for z, x, c in CTX]


SWAP_CORE = [(i, i ^ 1) for i in range(32)]
SWAP_ZL = [(i, i ^ 4) for i in range(8)]


def shift_y(k):
    return [(i, (i // 4) * 4 + (i + k) % 4) for i in range(8)]


def split3(value):
    high = value.astype(jnp.bfloat16).astype(jnp.float32)
    rest = value - high
    middle = rest.astype(jnp.bfloat16).astype(jnp.float32)
    low = (rest - middle).astype(jnp.bfloat16).astype(jnp.float32)
    return high, middle, low


def scores_of(keys, query):
    return lax.dot_general(
        keys, query, (((1,), (1,)), ((), ())), preferred_element_type=jnp.float32
    )


def weighted(values, weights):
    return lax.dot_general(
        values, weights, (((0,), (0,)), ((), ())), preferred_element_type=jnp.float32
    )


def fold(array, op):
    return functools.reduce(op, [array[i : i + 8] for i in range(0, array.shape[0], 8)])


def head_queries(refs, extra):
    lower = lax.broadcasted_iota(jnp.int32, (256, LANES), 1) < 64
    pair = jnp.concatenate([r[...] for r in refs], axis=0).astype(jnp.float32)
    a, b = pair[:, 128:256], pair[:, 256:384]
    marks = extra[...].astype(jnp.float32)
    a_turned, b_turned = pltpu.roll(a, 64, 1), pltpu.roll(b, 64, 1)
    even = [pair[:, :128], jnp.where(lower, a, marks)]
    odd = [jnp.where(lower, a_turned, b_turned), jnp.where(lower, b_turned, marks)]
    return [jnp.concatenate(q, axis=1).astype(jnp.bfloat16) for q in (even, odd)]


def attend_kernel(*refs):
    query_refs, extra, sources, lift_ref, kv_own = refs[:5], refs[5], refs[6:8], refs[8], refs[9]
    outs, (stats, score_buf, max_buf, lifted, query_buf, value_buf) = refs[10:17], refs[17:]
    step = pl.program_id(0)
    steps = HEADS // 2
    sizes = [sum(hi - lo for _, lo, hi in chunk) for chunk in CHUNKS]
    spans = [slice(sum(sizes[:i]), sum(sizes[: i + 1])) for i in range(len(sizes))]
    row = lax.broadcasted_iota(jnp.int32, (LANES, 256), 0)

    def tail_of(number):
        return jnp.concatenate([sources[i][a:b, LATENT:] for i, a, b in CHUNKS[number]], axis=0)

    def taken(number, slot, at):
        parts = [
            lifted[slot, a:b, at : at + 128] if i else kv_own[a:b, at : at + 128]
            for i, a, b in CHUNKS[number]
        ]
        return jnp.concatenate(parts, axis=0)

    def lift(rows, slot):
        product = jnp.dot(
            sources[1][rows, :LATENT], lift_ref[...], preferred_element_type=jnp.float32
        )
        lifted[slot, rows] = product.astype(jnp.bfloat16)

    def keep_queries(slot):
        for side, query in enumerate(head_queries(query_refs, extra)):
            query_buf[slot, side] = query

    def finish(top, total, result, head):
        column = pl.multiple_of(head * VDIM, VDIM)
        result = result.T.astype(jnp.bfloat16)
        for out, lo, hi in zip(outs, SPLIT, SPLIT[1:]):
            out[:, pl.ds(column, VDIM)] = result[lo:hi]
        found = stats[...]
        for i, part in enumerate(split3(top) + split3(total)):
            found = jnp.where(row == head + HEADS * i, part, found)
        stats[...] = found

    def phase(side, done_head, slot, lifts):
        done = 1 if side is None else 1 - side
        lifts = list(lifts)
        top = jnp.max(max_buf[done], axis=0, keepdims=True)
        total = jnp.zeros((8, 256), jnp.float32)
        result = jnp.zeros((VDIM, 256), jnp.float32)
        highest = jnp.full((8, 256), -jnp.inf, jnp.float32)
        for number, here in enumerate(spans):
            weights = jnp.exp2((score_buf[done, here] - top) * EXP2_SCALE)
            total += fold(weights, jnp.add)
            weights = weights.astype(jnp.bfloat16)
            if lifts and number == 1:
                lift(lifts.pop(0), 1 - slot)
            values = taken(number, slot, 128) if side == 1 else value_buf[here]
            result += weighted(values, weights)
            if side is not None:
                keys = jnp.concatenate([taken(number, slot, side * 256), tail_of(number)], axis=1)
                scores = scores_of(keys, query_buf[slot, side])
                score_buf[side, here] = scores
                highest = jnp.maximum(highest, fold(scores, jnp.maximum))
                if side == 1:
                    value_buf[here] = taken(number, slot, 384)
        for rows in lifts:
            lift(rows, 1 - slot)
        if side is not None:
            max_buf[side] = highest
        finish(top, jnp.sum(total, axis=0, keepdims=True), result, done_head)

    @pl.when(step == 0)
    def _():
        keep_queries(0)
        for rows in LIFTS:
            lift(rows, 0)

    for parity in range(2):

        @pl.when((step > 0) & (step < steps) & (step % 2 == parity))
        def _():
            phase(0, jnp.maximum(step * 2 - 3, 0), 1 - parity, LIFTS[:1])
            phase(1, step * 2 - 2, 1 - parity, LIFTS[1:])
            keep_queries(parity)

    @pl.when(step == steps)
    def _():
        slot = (steps - 1) % 2
        phase(0, HEADS - 3, slot, ())
        phase(1, HEADS - 2, slot, ())
        phase(None, HEADS - 1, slot, ())
        packed = jnp.where(row < 6 * HEADS, stats[...], 0.0).T.astype(jnp.bfloat16)
        for out, lo, hi in zip(outs, SPLIT, SPLIT[1:]):
            out[:, HEADS * VDIM :] = packed[lo:hi]


def attend(chunks, extra, sources, latent_up, kv_own):
    steps = HEADS // 2

    def pair(i):
        return 0, jnp.minimum(i, steps - 1)

    def pair_before(i):
        return 0, jnp.maximum(i - 1, 0)

    def whole(i):
        return 0, 0

    total = sum(source.shape[0] for source in sources)
    return pl.pallas_call(
        attend_kernel,
        grid=(steps + 1,),
        out_shape=[packed_shape(hi - lo) for lo, hi in zip(SPLIT, SPLIT[1:])],
        in_specs=[pl.BlockSpec((a.shape[0], 384), pair) for a in chunks]
        + [pl.BlockSpec(a.shape, whole) for a in (extra, *sources)]
        + [pl.BlockSpec((LATENT, 512), pair)]
        + [pl.BlockSpec((kv_own.shape[0], 512), pair_before)],
        out_specs=[pl.BlockSpec((hi - lo, PACKED), whole) for lo, hi in zip(SPLIT, SPLIT[1:])],
        scratch_shapes=[
            pltpu.VMEM((LANES, 256), jnp.float32),
            pltpu.VMEM((2, total, 256), jnp.float32),
            pltpu.VMEM((2, 8, 256), jnp.float32),
            pltpu.VMEM((2, total - kv_own.shape[0], 512), jnp.bfloat16),
            pltpu.VMEM((2, 2, 256, 256), jnp.bfloat16),
            pltpu.VMEM((total, VDIM), jnp.bfloat16),
        ],
        name="attend",
        compiler_params=pltpu.CompilerParams(vmem_limit_bytes=48 * 1024 * 1024),
    )(*chunks, extra, *sources, latent_up, kv_own)


def merge(refs, spans):
    tops, totals = [], []
    for ref, (lo, hi) in zip(refs, spans):
        raw = ref[lo:hi, HEADS * VDIM :].astype(jnp.float32)
        joined = raw + pltpu.roll(raw, 112, 1) + pltpu.roll(raw, 96, 1)
        tops.append(joined)
        totals.append(pltpu.roll(joined, 80, 1))
    top = functools.reduce(jnp.maximum, tops)
    factors = [jnp.exp2((t - top) * EXP2_SCALE) for t in tops]
    total = functools.reduce(jnp.add, [f * t for f, t in zip(factors, totals)])
    values = []
    for head in range(HEADS):
        at = head * VDIM
        values.append(
            functools.reduce(
                jnp.add,
                [
                    f[:, head : head + 1] * ref[lo:hi, at : at + VDIM].astype(jnp.float32)
                    for f, ref, (lo, hi) in zip(factors, refs, spans)
                ],
            )
        )
    return values, top, total


def pack_stats(top, total):
    lane = lax.broadcasted_iota(jnp.int32, top.shape, 1)
    packed = jnp.zeros_like(top)
    for i, part in enumerate(split3(top) + split3(total)):
        here = (lane >= 16 * i) & (lane < 16 * i + 16)
        packed = jnp.where(here, pltpu.roll(part, 16 * i, 1) if i else part, packed)
    return packed.astype(jnp.bfloat16)


def store_merged(out, rows, merged):
    values, top, total = merged
    for head, value in enumerate(values):
        out[rows, head * VDIM : (head + 1) * VDIM] = value.astype(jnp.bfloat16)
    out[rows, HEADS * VDIM :] = pack_stats(top, total)


def first_merge_kernel(own1, own3, from_left, from_right, out1, out3):
    for out, own, other in ((out1, own1, from_left), (out3, own3, from_right)):
        store_merged(out, slice(0, 32), merge([own, other], [(0, 32)] * 2))


def second_merge_kernel(own, left_a, left_b, right_a, right_b, *outs):
    for i, out in enumerate(outs):
        lo, at = i * ROWS, (i % 2) * ROWS
        refs = [own, left_a, right_a] if i < 2 else [own, left_b, right_b]
        spans = [(lo, lo + ROWS)] + [(at, at + ROWS)] * 2
        store_merged(out, slice(0, ROWS), merge(refs, spans))


def last_merge_kernel(a, b, c, d, out):
    values, top, total = merge([a, b, c, d], [(0, ROWS)] * 4)
    for head, value in enumerate(values):
        out[:, head * VDIM : (head + 1) * VDIM] = (value / total[:, head : head + 1]).astype(
            jnp.bfloat16
        )


def call(kernel, shapes, *args):
    return pl.pallas_call(
        kernel,
        out_shape=shapes,
        compiler_params=pltpu.CompilerParams(vmem_limit_bytes=32 * 1024 * 1024),
    )(*args)


def packed_shape(rows):
    return jax.ShapeDtypeStruct((rows, PACKED), jnp.bfloat16)


def shards(queries, cache, cache_len, new_latents, prefix_len, latent_up):
    bf16 = jnp.bfloat16
    me = lax.axis_index("ctx")
    my_z, my_x, my_core = me // 8, (me // 2) % 4, me % 2

    with jax.named_scope("mark_new"):
        mark = jnp.arange(64, dtype=jnp.int32)[None, :]
        new_row = jnp.arange(ROWS, dtype=jnp.int32)[:, None]
        new_wide = jnp.concatenate(
            [new_latents, (mark == 1 + my_core * ROWS + new_row).astype(bf16)], axis=1
        )
    with jax.named_scope("first_hop"):
        above = lax.ppermute(queries, "ctx", shift_z(-1))
        below = lax.ppermute(queries, "ctx", shift_z(1))
        up = lax.ppermute(cache, "head", shift_y(-1))
        down = lax.ppermute(cache, "head", shift_y(1))
    above, below, up, down = lax.optimization_barrier((above, below, up, down))
    with jax.named_scope("second_hop"):
        half = queries.shape[1] // 2
        across = [
            lax.ppermute(above[:, :half], "ctx", shift_z(-1)),
            lax.ppermute(below[:, half:], "ctx", shift_z(1)),
        ]
        chunk0 = jnp.concatenate(
            [queries, above, jnp.concatenate(across, axis=1), below], axis=0
        )
        up2 = lax.ppermute(up[:48], "head", shift_y(-1))
        down2 = lax.ppermute(down[48:], "head", shift_y(1))
        near = jnp.concatenate([cache, up, down], axis=0)
        there_near = lax.ppermute(near, "head", SWAP_ZL)
        opposite = jnp.concatenate([up2, down2], axis=0)
    chunk0, opposite = lax.optimization_barrier((chunk0, opposite))
    with jax.named_scope("third_hop"):
        chunk1 = lax.ppermute(chunk0, "ctx", shift_x(-1))
        chunk3 = lax.ppermute(chunk0, "ctx", shift_x(1))
        there_opposite = lax.ppermute(opposite, "head", SWAP_ZL)
    with jax.named_scope("mark_cache"):
        rows, head = cache.shape[0], lax.axis_index("head")
        index = jnp.arange(8 * rows, dtype=jnp.int32)
        turn = (index // rows) % 4
        y_from = (head + jnp.where(turn < 2, turn, 5 - turn)) % 4
        zl_from = (head // 4 + index // (4 * rows)) % 2
        place = (zl_from * 4 + y_from) * rows + index % rows
        hidden = jnp.where(place < cache_len[0], 0.0, HIDDEN).astype(bf16)
        hidden = jnp.where(jnp.arange(64)[None, :] == 0, hidden[:, None], 0.0).astype(bf16)
        block = jnp.concatenate([jnp.concatenate([near, opposite, there_near, there_opposite], axis=0), hidden], axis=1)
        own = jnp.concatenate([block, new_wide], axis=0)
    with jax.named_scope("fourth_hop"):
        far = lax.ppermute(own, "ctx", SWAP_CORE)
        chunk2a = lax.ppermute(chunk1[:32], "ctx", shift_x(-1))
        chunk2b = lax.ppermute(chunk3[32:], "ctx", shift_x(1))
    with jax.named_scope("marks"):
        row = jnp.arange(256, dtype=jnp.int32)[:, None]
        row_z = (my_z + (row // 16) % 4) % 4
        row_x = (my_x + row // 64) % 4
        query_index = ((row_z * 8 + row_x * 2 + my_core) * ROWS) + row % 16
        lane = jnp.arange(LANES, dtype=jnp.int32)[None, :] % 64
        new_at = lane - 1
        new_index = ((my_z * 8 + my_x * 2 + new_at // 16) * ROWS) + new_at % 16
        visible = (new_index <= query_index) | (new_index < prefix_len[0])
        extra = jnp.where(
            lane == 0, 1.0, jnp.where((lane > 32) | visible, 0.0, HIDDEN)
        ).astype(bf16)

    with jax.named_scope("lift_own"):
        kv_own = jnp.dot(own[:, :LATENT], latent_up, preferred_element_type=jnp.float32).astype(bf16)
    sources = [own, far]
    chunks = [chunk0, chunk1, chunk2a, chunk2b, chunk3]
    with jax.named_scope("attend"):
        out0, out1a, out1b, out2a, out2b, out3a, out3b = attend(
            chunks, extra, sources, latent_up, kv_own
        )
    with jax.named_scope("reduce_x"):
        left2 = lax.ppermute(out2a, "ctx", shift_x(1))
        right2 = lax.ppermute(out2b, "ctx", shift_x(-1))
        left_b = lax.ppermute(out1b, "ctx", shift_x(1))
        right_a = lax.ppermute(out3a, "ctx", shift_x(-1))
        sum1, sum3 = call(first_merge_kernel, [packed_shape(32)] * 2, out1a, out3b, left2, right2)
        left_a = lax.ppermute(sum1, "ctx", shift_x(1))
        right_b = lax.ppermute(sum3, "ctx", shift_x(-1))
        shapes = [packed_shape(ROWS)] * 4
        parts = call(second_merge_kernel, shapes, out0, left_a, left_b, right_a, right_b)
    with jax.named_scope("reduce_z"):
        arrived = [lax.ppermute(parts[k], "ctx", shift_z(k)) for k in (2, 1, 3)]
        return call(
            last_merge_kernel,
            jax.ShapeDtypeStruct((ROWS, HEADS * VDIM), bf16),
            parts[0],
            *arrived,
        )


def solution(mesh):
    placed = (
        P("ctx", "head"),
        P(("ctx", "head"), None),
        P("ctx"),
        P("ctx", None),
        P(),
        P(None, "head"),
    )
    return jax.shard_map(
        shards, mesh=mesh, in_specs=placed, out_specs=P("ctx", "head"), check_vma=False
    )
```
